256 devices in a mesh: dp: 16 (over y_lo, x, core), owner: 16 (over y_hi, z).
Axes of the slice: x: 4, y: 4 (y_hi: 2, y_lo: 2; y = y_hi * 2 + y_lo), z: 8, core: 2. Of those that a mesh axis runs over, the one named last changes fastest.
Arguments:
- acts: bfloat16 [16, 4096, 2560], P('owner', 'dp'), may hold values from -6 to 6
- outgrads: bfloat16 [16, 4096, 2560], P('owner', 'dp'), may hold values from -6 to 6
Outputs:
- update: bfloat16 [16, 2560, 2560], P(None, 'dp', 'owner')
The draws below stay inside these ranges and needn't reach their ends.
All inputs are finite; a program needn't handle non-finite values.
Results may differ from the reference program's by a relative error of at most 0.0057.
Values may be sent and summed in bfloat16 or wider, within the bound.
No kernel may reach another device: no remote copies, remote signals or barrier semaphores. Data moves between devices by JAX's collectives and lax.ppermute only.
A program may use at most 128 MiB of HBM per device.

```python
import math
import jax
import jax.numpy as jnp
from jax import lax

D = 2560
BLK = 128
NS_ITERS = 4
NBLK = 20
LAYERS = 16
TOKENS = 4096


def shard_levels(own_key, shape, pieces, smallest, top_value):
    level, own = 1.0, jax.random.fold_in(own_key, 6)
    for position, parts in pieces:
        heights = jnp.exp(jax.random.uniform(jax.random.fold_in(own, position), (parts,), jnp.float32, smallest / len(pieces), top_value / len(pieces)))
        level = level * jnp.repeat(heights, shape[position] // parts).reshape([-1 if axis == position else 1 for axis in range(len(shape))])
    return level


def gaussian(key, dims, spread, limit, shards=(), held_as=jnp.bfloat16):
    result = jax.random.normal(key, dims, jnp.float32) * spread
    if len(shards) > 0:
        result = shard_levels(key, dims, shards, -0.22, 0.18) * result
    return jnp.clip(result, min=-limit, max=limit).astype(held_as)


def setup_inputs(seed: int = 0) -> dict:
    arg_keys = jax.random.split(jax.random.key(seed), 3)
    return {
        "acts": gaussian(arg_keys[0], (LAYERS, TOKENS, D), 1.0, 6.0, ((0, 16), (1, 16))),
        "outgrads": gaussian(arg_keys[1], (LAYERS, TOKENS, D), 1.0, 6.0, ((0, 16), (1, 16))),
    }


damping = 0.1

def newton(matrix):
    row_sums = lax.optimization_barrier(jnp.sum(jnp.abs(matrix), axis=2))
    largest = lax.optimization_barrier(jnp.max(row_sums, axis=1))
    identity = jnp.eye(matrix.shape[1], dtype=jnp.float32)
    iterate = identity[None] / largest[:, None, None]
    for step_index in range(NS_ITERS):
        product = jnp.einsum('bij,bjk->bik', iterate, matrix, precision=lax.Precision.HIGHEST)
        iterate = 2.0 * iterate - jnp.einsum('bij,bjk->bik', product, iterate, precision=lax.Precision.HIGHEST)
    return iterate

def factor(values):
    blocks = values.astype(jnp.float32).reshape(TOKENS, NBLK, BLK)
    grams = jnp.einsum('tbi,tbj->bij', blocks, blocks, precision=lax.Precision.HIGHEST)
    identity = jnp.eye(BLK, dtype=jnp.float32)
    return grams / TOKENS + damping * identity[None]

def precondition(values, inverse):
    blocks = values.astype(jnp.float32).reshape(TOKENS, NBLK, BLK)
    mapped = jnp.einsum('tbi,bij->tbj', blocks, inverse, precision=lax.Precision.HIGHEST)
    return mapped.reshape(TOKENS, D).astype(jnp.bfloat16)

def reference(acts, outgrads):

    def layer_update(pair):
        act_now, grad_now = pair
        act_inverse = newton(factor(act_now))
        grad_inverse = newton(factor(grad_now))
        act_tilde = precondition(act_now, act_inverse)
        grad_tilde = precondition(grad_now, grad_inverse)
        summed = jnp.dot(act_tilde.T, grad_tilde, preferred_element_type=jnp.float32)
        return (summed / math.sqrt(TOKENS)).astype(jnp.bfloat16)
    return lax.map(layer_update, (acts, outgrads))
```

```python
import functools
import math

import jax
import jax.numpy as jnp
from jax import lax
from jax.experimental import pallas as pl
from jax.experimental.pallas import tpu as pltpu
from jax.sharding import PartitionSpec as P

BLK = 128
DAMPING = 0.1
TOKENS = 4096
D = 2560
HALF = D // 2
QUART = D // 4
NB = QUART // BLK
OUT = 160
PACK = 208
AXES = ("dp", "owner")
F32 = jnp.float32
BF16 = jnp.bfloat16
HI = lax.Precision.HIGHEST
VMEM = 60 * 2**20


def params():
    return pltpu.CompilerParams(vmem_limit_bytes=VMEM)


def pairs(move):
    result = []
    for d in range(16):
        for o in range(16):
            y, x, c, p = move(d // 8, (d // 2) % 4, d % 2, o)
            result.append((d * 16 + o, (y * 8 + x * 2 + c) * 16 + p))
    return result


def send(value, move):
    return lax.ppermute(value, AXES, pairs(move))


def swap_y(y, x, c, o):
    return 1 - y, x, c, o


def swap_core(y, x, c, o):
    return y, x, 1 - c, o


def swap_y_core(y, x, c, o):
    return 1 - y, x, 1 - c, o


def plus_x(y, x, c, o):
    return y, (x + 1) % 4, c, o


def minus_x(y, x, c, o):
    return y, (x + 3) % 4, c, o


def far_x(y, x, c, o):
    return y, (x + 2) % 4, c, o


def columns(value, index, width):
    return lax.dynamic_slice(value, (0, index * width), (value.shape[0], width))


def accumulate_kernel(plan, n_g, first, *refs):
    n = len(plan)
    a_refs, g_refs, refs = refs[:n], refs[n : n + n_g], refs[n + n_g :]
    if not first:
        prev_s, prev_m, refs = refs[0], refs[1], refs[2:]
    s_ref, m_ref = refs
    col = pl.ds(pl.multiple_of(pl.program_id(0) * BLK, BLK), BLK)
    s = jnp.zeros((BLK, QUART), F32) if first else prev_s[...]
    m_a = jnp.zeros((BLK, BLK), F32) if first else prev_m[0, 0]
    m_g = jnp.zeros((BLK, BLK), F32) if first else prev_m[0, 1]
    for a_ref, parts in zip(a_refs, plan):
        row = 0
        for which, start, size in parts:
            a = a_ref[row : row + size, :]
            g = g_refs[which][start : start + size, :]
            part = g_refs[which][start : start + size, col]
            at = a.T
            both = jnp.dot(at, jnp.concatenate([g, a], axis=1), preferred_element_type=F32)
            s += both[:, :QUART]
            m_a += both[:, QUART:]
            m_g += jnp.dot(part.T, part, preferred_element_type=F32)
            row += size
    s_ref[...] = s
    m_ref[0, 0] = m_a
    m_ref[0, 1] = m_g


def accumulate(a_list, plan, g_list, prev=None):
    s_spec = pl.BlockSpec((BLK, QUART), lambda i: (i, 0))
    m_spec = pl.BlockSpec((1, 2, BLK, BLK), lambda i: (i, 0, 0, 0))
    a_specs = [pl.BlockSpec((a.shape[0], BLK), lambda i: (0, i)) for a in a_list]
    g_specs = [pl.BlockSpec(g.shape, lambda i: (0, 0)) for g in g_list]
    extra = [] if prev is None else list(prev)
    tok = sum(a.shape[0] for a in a_list)
    return pl.pallas_call(
        functools.partial(accumulate_kernel, plan, len(g_list), prev is None),
        grid=(NB,),
        in_specs=a_specs + g_specs + ([s_spec, m_spec] if extra else []),
        out_specs=[s_spec, m_spec],
        out_shape=[
            jax.ShapeDtypeStruct((QUART, QUART), F32),
            jax.ShapeDtypeStruct((NB, 2, BLK, BLK), F32),
        ],
        compiler_params=params(),
        cost_estimate=pl.CostEstimate(
            flops=2 * tok * QUART * (QUART + 2 * BLK), bytes_accessed=tok * QUART * 4 + 8 * QUART * QUART, transcendentals=0
        ),
        name="accumulate",
    )(*a_list, *g_list, *extra)


def split(value):
    high = value.astype(BF16)
    return high, (value - high.astype(F32)).astype(BF16)


def dot_split(a, b):
    a_high, a_low = split(a)
    b_high, b_low = split(b)
    wide = jnp.concatenate([b_high, b_low], axis=1)
    both = jnp.dot(
        jnp.concatenate([a_high, a_low], axis=1),
        jnp.concatenate([wide, wide], axis=0),
        preferred_element_type=F32,
    )
    return both[:, :BLK] + both[:, BLK:]


def dot_left(a, b):
    a_high, a_low = split(a)
    b_high, b_low = split(b)
    total = jnp.dot(
        jnp.concatenate([a_high, a_low], axis=1),
        jnp.concatenate([b_high, b_high], axis=0),
        preferred_element_type=F32,
    )
    return total + jnp.dot(a_high, b_low, preferred_element_type=F32)


def finish_kernel(core, s_prev, m_prev, *refs):
    keep, give, inv, upd = refs[6:]
    tok = refs[2].shape[0]
    late = [(refs[n // 2], (n % 2) * tok, refs[2 + n]) for n in range(4)]
    rows = lax.broadcasted_iota(jnp.int32, (BLK, BLK), 0)
    cols = lax.broadcasted_iota(jnp.int32, (BLK, BLK), 1)
    eye = (rows == cols).astype(F32)
    errs, scales = [], []
    for i in range(NB):
        blk = slice(i * BLK, (i + 1) * BLK)
        total = s_prev[blk, :]
        m_a, m_g = m_prev[i, 0], m_prev[i, 1]
        for a_ref, row, g_ref in late:
            a, g = a_ref[row : row + tok, blk], g_ref[:, blk]
            at = a.T
            total += jnp.dot(at, g_ref[...], preferred_element_type=F32)
            m_a += jnp.dot(at, a, preferred_element_type=F32)
            m_g += jnp.dot(g.T, g, preferred_element_type=F32)
        upd[blk, :] = total
        for m in (m_a, m_g):
            m = m * (1.0 / TOKENS) + DAMPING * eye
            bound = jnp.max(jnp.sum(jnp.abs(m), axis=0, keepdims=True), axis=1, keepdims=True)
            scale = 1.0 / bound
            errs.append(eye - m * scale)
            scales.append(scale)
    prods = [eye + e for e in errs]
    errs = [dot_split(e, e) for e in errs]
    for step in range(3):
        if step < 2:
            both = [dot_split(jnp.concatenate([p, e], axis=0), e) for p, e in zip(prods, errs)]
            prods = [p + t[:BLK] for p, t in zip(prods, both)]
            errs = [t[BLK:] for t in both]
        else:
            prods = [p + dot_split(p, e) for p, e in zip(prods, errs)]
    for n in range(2 * NB):
        inv[n] = prods[n] * scales[n]
    for i in range(NB):
        blk = slice(i * BLK, (i + 1) * BLK)
        upd[blk, :] = dot_left(inv[2 * i].T, upd[blk, :])
    for j in range(NB):
        blk = slice(j * BLK, (j + 1) * BLK)
        upd[:, blk] = dot_split(upd[:, blk], inv[2 * j + 1]) * (1.0 / math.sqrt(TOKENS))
    for out, parity in ((keep, core[0]), (give, 1 - core[0])):
        for b in range(2):
            start = pl.multiple_of((2 * b + parity) * OUT, 32)
            strip = upd[pl.ds(start, OUT), :]
            for j in range(4):
                piece = strip[:, j * OUT : (j + 1) * OUT]
                tail = piece[:, BLK:]
                packed = jnp.concatenate([tail[q * 40 : (q + 1) * 40] for q in range(4)], axis=1)
                packed = jnp.concatenate([packed, jnp.zeros((8, BLK), F32)], axis=0)
                out[b, j, :OUT, :] = piece[:, :BLK].astype(BF16)
                out[b, j, OUT:, :] = packed.astype(BF16)


def finish(core, sums, a_late, g_arrays):
    tok = a_late[0].shape[0] // 2

    def whole(shape):
        return pl.BlockSpec(shape, lambda i, c: (0,) * len(shape))

    out = jax.ShapeDtypeStruct((2, 4, PACK, BLK), BF16)
    return pl.pallas_call(
        finish_kernel,
        grid_spec=pltpu.PrefetchScalarGridSpec(
            num_scalar_prefetch=1,
            grid=(1,),
            in_specs=[whole(v.shape) for v in (*sums, *a_late)] + [pl.BlockSpec((tok, QUART), lambda i, c: (3, 0))] * 4,
            out_specs=[whole(out.shape)] * 2,
            scratch_shapes=[pltpu.VMEM((2 * NB, BLK, BLK), F32), pltpu.VMEM((QUART, QUART), F32)],
        ),
        out_shape=[out] * 2,
        compiler_params=params(),
        cost_estimate=pl.CostEstimate(flops=2 * 10**9, bytes_accessed=5 * 10**6, transcendentals=0),
        name="finish",
    )(core, *sums, *a_late, *g_arrays)


def unpack_kernel(src, dst):
    for l in range(8):
        tail = src[l, OUT:, :].astype(F32)
        ext = jnp.concatenate([tail[:40, q * 32 : (q + 1) * 32] for q in range(4)], axis=0)
        dst[l, :, :BLK] = src[l, :OUT, :]
        dst[l, :, BLK:] = ext.astype(BF16)


def unpack(packed):
    return pl.pallas_call(
        unpack_kernel,
        grid=(2,),
        in_specs=[pl.BlockSpec((8, PACK, BLK), lambda i: (i, 0, 0))],
        out_specs=pl.BlockSpec((8, OUT, OUT), lambda i: (i, 0, 0)),
        out_shape=jax.ShapeDtypeStruct((16, OUT, OUT), BF16),
        compiler_params=params(),
        name="unpack",
    )(packed)


def after(value, *done):
    return lax.optimization_barrier((value, *done))[0]


def local(acts, outgrads):
    d = lax.axis_index("dp")
    y, x, c = d // 8, (d // 2) % 4, d % 2
    place = jnp.stack([c, x]).astype(jnp.int32)
    a_now, g_now = acts[0], outgrads[0]
    tok = a_now.shape[0]

    g_left = send(columns(g_now, (x + 1) % 4, QUART), plus_x)
    g_right = send(columns(g_now, (x + 3) % 4, QUART), minus_x)
    g_far = send(columns(g_now, (x + 2) % 4, QUART), far_x)
    mate = [
        send(columns(a_now, 2 * (1 - y) + c, QUART), swap_y),
        send(columns(a_now, 2 * (1 - y) + 1 - c, QUART), swap_y_core),
    ]
    own = [columns(a_now, 2 * y + c, QUART), send(columns(a_now, 2 * y + 1 - c, QUART), swap_core)]

    own_all = jnp.concatenate(own, axis=0)
    g_all = jnp.concatenate([columns(g_now, x, QUART), g_left, g_right, after(g_far, own_all)], axis=0)
    g_mate = send(after(g_all, *mate), swap_y)
    g_other = send(g_all, swap_core)

    mate_all = jnp.concatenate(mate, axis=0)
    own_left, own_right = send(own_all, plus_x), send(own_all, minus_x)
    mate_left, mate_right = send(mate_all, plus_x), send(mate_all, minus_x)
    own_far = send(own_left, plus_x)
    mate_far = send(mate_right, minus_x)
    g_mate_other = send(after(g_mate, own_left, own_right, mate_left, mate_right), swap_core)
    plan = [[(n, k * tok, tok), (n + 1, k * tok, tok)] for n in (0, 2) for k in range(3)]
    sums = accumulate(
        [own_all, own_left, own_right, mate_all, mate_left, mate_right], plan, [g_all, g_other, g_mate, g_mate_other]
    )
    keep, give = finish(place, sums, [own_far, mate_far], [g_all, g_other, g_mate, g_mate_other])
    recv = send(give, swap_core)
    got = []
    for k, move in enumerate([None, plus_x, far_x, minus_x]):
        target = (x + k) % 4
        strip = jnp.where(
            target // 2 == c,
            lax.dynamic_index_in_dim(keep, target % 2, 0, False),
            lax.dynamic_index_in_dim(recv, target % 2, 0, False),
        )
        got.append(strip if move is None else send(strip, move))
    pieces = jnp.zeros((16, PACK, BLK), BF16)
    for k in range(4):
        pieces = lax.dynamic_update_slice(pieces, got[k], (((x + 4 - k) % 4) * 4, 0, 0))
    return unpack(lax.all_to_all(pieces, "owner", split_axis=0, concat_axis=0, tiled=True))


def solution(mesh):
    return jax.shard_map(
        local,
        mesh=mesh,
        in_specs=(P("owner", "dp", None), P("owner", "dp", None)),
        out_specs=P(None, "dp", "owner"),
        check_vma=False,
    )
```

```python
import functools
import math

import jax
import jax.numpy as jnp
from jax import lax
from jax.experimental import pallas as pl
from jax.experimental.pallas import tpu as pltpu
from jax.sharding import PartitionSpec as P

BLK = 128
DAMPING = 0.1
TOKENS = 4096
D = 2560
HALF = D // 2
QUART = D // 4
NB = QUART // BLK
OUT = 160
PACK = 208
AXES = ("dp", "owner")
F32 = jnp.float32
BF16 = jnp.bfloat16
HI = lax.Precision.HIGHEST
VMEM = 28 * 2**20


def params():
    return pltpu.CompilerParams(vmem_limit_bytes=VMEM)


def pairs(move):
    result = []
    for d in range(16):
        for o in range(16):
            y, x, c, p = move(d // 8, (d // 2) % 4, d % 2, o)
            result.append((d * 16 + o, (y * 8 + x * 2 + c) * 16 + p))
    return result


def send(value, move):
    return lax.ppermute(value, AXES, pairs(move))


def swap_y(y, x, c, o):
    return 1 - y, x, c, o


def swap_core(y, x, c, o):
    return y, x, 1 - c, o


def swap_y_core(y, x, c, o):
    return 1 - y, x, 1 - c, o


def plus_x(y, x, c, o):
    return y, (x + 1) % 4, c, o


def minus_x(y, x, c, o):
    return y, (x + 3) % 4, c, o


def far_x(y, x, c, o):
    return y, (x + 2) % 4, c, o


def columns(value, index, width):
    return lax.dynamic_slice(value, (0, index * width), (value.shape[0], width))


def accumulate_kernel(plan, n_g, first, *refs):
    n = len(plan)
    a_refs, g_refs, refs = refs[:n], refs[n : n + n_g], refs[n + n_g :]
    if not first:
        prev_s, prev_m, refs = refs[0], refs[1], refs[2:]
    s_ref, m_ref = refs
    col = pl.ds(pl.multiple_of(pl.program_id(0) * BLK, BLK), BLK)
    s = jnp.zeros((BLK, QUART), F32) if first else prev_s[...]
    m_a = jnp.zeros((BLK, BLK), F32) if first else prev_m[0, 0]
    m_g = jnp.zeros((BLK, BLK), F32) if first else prev_m[0, 1]
    for a_ref, parts in zip(a_refs, plan):
        row = 0
        for which, start, size in parts:
            a = a_ref[row : row + size, :]
            g = g_refs[which][start : start + size, :]
            part = g_refs[which][start : start + size, col]
            at = a.T
            both = jnp.dot(at, jnp.concatenate([g, a], axis=1), preferred_element_type=F32)
            s += both[:, :QUART]
            m_a += both[:, QUART:]
            m_g += jnp.dot(part.T, part, preferred_element_type=F32)
            row += size
    s_ref[...] = s
    m_ref[0, 0] = m_a
    m_ref[0, 1] = m_g


def accumulate(a_list, plan, g_list, prev=None):
    s_spec = pl.BlockSpec((BLK, QUART), lambda i: (i, 0))
    m_spec = pl.BlockSpec((1, 2, BLK, BLK), lambda i: (i, 0, 0, 0))
    a_specs = [pl.BlockSpec((a.shape[0], BLK), lambda i: (0, i)) for a in a_list]
    g_specs = [pl.BlockSpec(g.shape, lambda i: (0, 0)) for g in g_list]
    extra = [] if prev is None else list(prev)
    tok = sum(a.shape[0] for a in a_list)
    return pl.pallas_call(
        functools.partial(accumulate_kernel, plan, len(g_list), prev is None),
        grid=(NB,),
        in_specs=a_specs + g_specs + ([s_spec, m_spec] if extra else []),
        out_specs=[s_spec, m_spec],
        out_shape=[
            jax.ShapeDtypeStruct((QUART, QUART), F32),
            jax.ShapeDtypeStruct((NB, 2, BLK, BLK), F32),
        ],
        compiler_params=params(),
        cost_estimate=pl.CostEstimate(
            flops=2 * tok * QUART * (QUART + 2 * BLK), bytes_accessed=tok * QUART * 4 + 8 * QUART * QUART, transcendentals=0
        ),
        name="accumulate",
    )(*a_list, *g_list, *extra)


def split(value):
    high = value.astype(BF16)
    return high, (value - high.astype(F32)).astype(BF16)


def dot_split(a, b):
    a_high, a_low = split(a)
    b_high, b_low = split(b)
    wide = jnp.concatenate([b_high, b_low], axis=1)
    both = jnp.dot(
        jnp.concatenate([a_high, a_low], axis=1),
        jnp.concatenate([wide, wide], axis=0),
        preferred_element_type=F32,
    )
    return both[:, :BLK] + both[:, BLK:]


def dot_left(a, b):
    a_high, a_low = split(a)
    b_high, b_low = split(b)
    total = jnp.dot(
        jnp.concatenate([a_high, a_low], axis=1),
        jnp.concatenate([b_high, b_high], axis=0),
        preferred_element_type=F32,
    )
    return total + jnp.dot(a_high, b_low, preferred_element_type=F32)


def finish_kernel(core, s_prev, m_prev, *refs):
    keep, give, inv, upd = refs[6:]
    tok = refs[2].shape[0]
    late = [(refs[n // 2], (n % 2) * tok, refs[2 + n]) for n in range(4)]
    rows = lax.broadcasted_iota(jnp.int32, (BLK, BLK), 0)
    cols = lax.broadcasted_iota(jnp.int32, (BLK, BLK), 1)
    eye = (rows == cols).astype(F32)
    errs, scales = [], []
    for i in range(NB):
        blk = slice(i * BLK, (i + 1) * BLK)
        total = s_prev[blk, :]
        m_a, m_g = m_prev[i, 0], m_prev[i, 1]
        for a_ref, row, g_ref in late:
            a, g = a_ref[row : row + tok, blk], g_ref[:, blk]
            at = a.T
            total += jnp.dot(at, g_ref[...], preferred_element_type=F32)
            m_a += jnp.dot(at, a, preferred_element_type=F32)
            m_g += jnp.dot(g.T, g, preferred_element_type=F32)
        upd[blk, :] = total
        for m in (m_a, m_g):
            m = m * (1.0 / TOKENS) + DAMPING * eye
            bound = jnp.max(jnp.sum(jnp.abs(m), axis=0, keepdims=True), axis=1, keepdims=True)
            scale = 1.0 / bound
            errs.append(eye - m * scale)
            scales.append(scale)
    prods = [eye + e for e in errs]
    errs = [dot_split(e, e) for e in errs]
    for step in range(3):
        if step < 2:
            both = [dot_split(jnp.concatenate([p, e], axis=0), e) for p, e in zip(prods, errs)]
            prods = [p + t[:BLK] for p, t in zip(prods, both)]
            errs = [t[BLK:] for t in both]
        else:
            prods = [p + dot_split(p, e) for p, e in zip(prods, errs)]
    for n in range(2 * NB):
        inv[n] = prods[n] * scales[n]
    for i in range(NB):
        blk = slice(i * BLK, (i + 1) * BLK)
        upd[blk, :] = dot_left(inv[2 * i].T, upd[blk, :])
    for j in range(NB):
        blk = slice(j * BLK, (j + 1) * BLK)
        upd[:, blk] = dot_split(upd[:, blk], inv[2 * j + 1]) * (1.0 / math.sqrt(TOKENS))
    for out, parity in ((keep, core[0]), (give, 1 - core[0])):
        for b in range(2):
            start = pl.multiple_of((2 * b + parity) * OUT, 32)
            strip = upd[pl.ds(start, OUT), :]
            for j in range(4):
                piece = strip[:, j * OUT : (j + 1) * OUT]
                tail = piece[:, BLK:]
                packed = jnp.concatenate([tail[q * 40 : (q + 1) * 40] for q in range(4)], axis=1)
                packed = jnp.concatenate([packed, jnp.zeros((8, BLK), F32)], axis=0)
                out[b, j, :OUT, :] = piece[:, :BLK].astype(BF16)
                out[b, j, OUT:, :] = packed.astype(BF16)


def finish(core, sums, a_late, g_arrays):
    tok = a_late[0].shape[0] // 2

    def whole(shape):
        return pl.BlockSpec(shape, lambda i, c: (0,) * len(shape))

    out = jax.ShapeDtypeStruct((2, 4, PACK, BLK), BF16)
    return pl.pallas_call(
        finish_kernel,
        grid_spec=pltpu.PrefetchScalarGridSpec(
            num_scalar_prefetch=1,
            grid=(1,),
            in_specs=[whole(v.shape) for v in (*sums, *a_late)] + [pl.BlockSpec((tok, QUART), lambda i, c: (3, 0))] * 4,
            out_specs=[whole(out.shape)] * 2,
            scratch_shapes=[pltpu.VMEM((2 * NB, BLK, BLK), F32), pltpu.VMEM((QUART, QUART), F32)],
        ),
        out_shape=[out] * 2,
        compiler_params=params(),
        cost_estimate=pl.CostEstimate(flops=2 * 10**9, bytes_accessed=5 * 10**6, transcendentals=0),
        name="finish",
    )(core, *sums, *a_late, *g_arrays)


def unpack_kernel(src, dst):
    for l in range(8):
        tail = src[l, OUT:, :].astype(F32)
        ext = jnp.concatenate([tail[:40, q * 32 : (q + 1) * 32] for q in range(4)], axis=0)
        dst[l, :, :BLK] = src[l, :OUT, :]
        dst[l, :, BLK:] = ext.astype(BF16)


def unpack(packed):
    return pl.pallas_call(
        unpack_kernel,
        grid=(2,),
        in_specs=[pl.BlockSpec((8, PACK, BLK), lambda i: (i, 0, 0))],
        out_specs=pl.BlockSpec((8, OUT, OUT), lambda i: (i, 0, 0)),
        out_shape=jax.ShapeDtypeStruct((16, OUT, OUT), BF16),
        compiler_params=params(),
        name="unpack",
    )(packed)


def after(value, *done):
    return lax.optimization_barrier((value, *done))[0]


def local(acts, outgrads):
    d = lax.axis_index("dp")
    y, x, c = d // 8, (d // 2) % 4, d % 2
    place = jnp.stack([c, x]).astype(jnp.int32)
    a_now, g_now = acts[0], outgrads[0]
    tok = a_now.shape[0]

    g_left = send(columns(g_now, (x + 1) % 4, QUART), plus_x)
    g_right = send(columns(g_now, (x + 3) % 4, QUART), minus_x)
    g_far = send(columns(g_now, (x + 2) % 4, QUART), far_x)
    swapped = send(jnp.concatenate([columns(a_now, 2 * half + 1 - c, QUART) for half in (y, 1 - y)], axis=0), swap_core)
    mate_all = send(jnp.concatenate([columns(a_now, 2 * (1 - y) + c, QUART), swapped[tok:]], axis=0), swap_y)
    own_all = jnp.concatenate([columns(a_now, 2 * y + c, QUART), swapped[:tok]], axis=0)

    g_all = jnp.concatenate([columns(g_now, x, QUART), g_left, g_right, g_far], axis=0)
    g_mate = send(after(g_all, mate_all), swap_y)
    g_other = send(g_all, swap_core)

    own_left, own_right = send(own_all, plus_x), send(own_all, minus_x)
    mate_left, mate_right = send(mate_all, plus_x), send(mate_all, minus_x)
    own_far = send(own_left, plus_x)
    mate_far = send(mate_right, minus_x)
    g_mate_other = send(after(g_mate, own_left, own_right, mate_left, mate_right), swap_core)
    plan = [[(n, k * tok, tok), (n + 1, k * tok, tok)] for n in (0, 2) for k in range(3)]
    sums = accumulate(
        [own_all, own_left, own_right, mate_all, mate_left, mate_right], plan, [g_all, g_other, g_mate, g_mate_other]
    )
    keep, give = finish(place, sums, [own_far, mate_far], [g_all, g_other, g_mate, g_mate_other])
    recv = send(give, swap_core)
    got = []
    for k, move in enumerate([None, plus_x, far_x, minus_x]):
        target = (x + k) % 4
        strip = jnp.where(
            target // 2 == c,
            lax.dynamic_index_in_dim(keep, target % 2, 0, False),
            lax.dynamic_index_in_dim(recv, target % 2, 0, False),
        )
        got.append(strip if move is None else send(strip, move))
    pieces = jnp.zeros((16, PACK, BLK), BF16)
    for k in range(4):
        pieces = lax.dynamic_update_slice(pieces, got[k], (((x + 4 - k) % 4) * 4, 0, 0))
    return unpack(lax.all_to_all(pieces, "owner", split_axis=0, concat_axis=0, tiled=True))


def solution(mesh):
    return jax.shard_map(
        local,
        mesh=mesh,
        in_specs=(P("owner", "dp", None), P("owner", "dp", None)),
        out_specs=P(None, "dp", "owner"),
        check_vma=False,
    )
```

```python
import functools
import math

import jax
import jax.numpy as jnp
from jax import lax
from jax.experimental import pallas as pl
from jax.experimental.pallas import tpu as pltpu
from jax.sharding import PartitionSpec as P

BLK = 128
DAMPING = 0.1
TOKENS = 4096
D = 2560
HALF = D // 2
QUART = D // 4
NB = QUART // BLK
OUT = 160
PACK = 208
AXES = ("dp", "owner")
F32 = jnp.float32
BF16 = jnp.bfloat16
HI = lax.Precision.HIGHEST
VMEM = 28 * 2**20


def params():
    return pltpu.CompilerParams(vmem_limit_bytes=VMEM)


def pairs(move):
    result = []
    for d in range(16):
        for o in range(16):
            y, x, c, p = move(d // 8, (d // 2) % 4, d % 2, o)
            result.append((d * 16 + o, (y * 8 + x * 2 + c) * 16 + p))
    return result


def send(value, move):
    return lax.ppermute(value, AXES, pairs(move))


def swap_y(y, x, c, o):
    return 1 - y, x, c, o


def swap_core(y, x, c, o):
    return y, x, 1 - c, o


def swap_y_core(y, x, c, o):
    return 1 - y, x, 1 - c, o


def plus_x(y, x, c, o):
    return y, (x + 1) % 4, c, o


def minus_x(y, x, c, o):
    return y, (x + 3) % 4, c, o


def far_x(y, x, c, o):
    return y, (x + 2) % 4, c, o


def columns(value, index, width):
    return lax.dynamic_slice(value, (0, index * width), (value.shape[0], width))


def accumulate_kernel(plan, n_g, first, *refs):
    n = len(plan)
    a_refs, g_refs, refs = refs[:n], refs[n : n + n_g], refs[n + n_g :]
    if not first:
        prev_s, prev_m, refs = refs[0], refs[1], refs[2:]
    s_ref, m_ref = refs
    col = pl.ds(pl.multiple_of(pl.program_id(0) * BLK, BLK), BLK)
    s = jnp.zeros((BLK, QUART), F32) if first else prev_s[...]
    m_a = jnp.zeros((BLK, BLK), F32) if first else prev_m[0, 0]
    m_g = jnp.zeros((BLK, BLK), F32) if first else prev_m[0, 1]
    for a_ref, parts in zip(a_refs, plan):
        row = 0
        for which, start, size in parts:
            a = a_ref[row : row + size, :]
            g = g_refs[which][start : start + size, :]
            part = g_refs[which][start : start + size, col]
            at = a.T
            both = jnp.dot(at, jnp.concatenate([g, a], axis=1), preferred_element_type=F32)
            s += both[:, :QUART]
            m_a += both[:, QUART:]
            m_g += jnp.dot(part.T, part, preferred_element_type=F32)
            row += size
    s_ref[...] = s
    m_ref[0, 0] = m_a
    m_ref[0, 1] = m_g


def accumulate(a_list, plan, g_list, prev=None):
    s_spec = pl.BlockSpec((BLK, QUART), lambda i: (i, 0))
    m_spec = pl.BlockSpec((1, 2, BLK, BLK), lambda i: (i, 0, 0, 0))
    a_specs = [pl.BlockSpec((a.shape[0], BLK), lambda i: (0, i)) for a in a_list]
    g_specs = [pl.BlockSpec(g.shape, lambda i: (0, 0)) for g in g_list]
    extra = [] if prev is None else list(prev)
    tok = sum(a.shape[0] for a in a_list)
    return pl.pallas_call(
        functools.partial(accumulate_kernel, plan, len(g_list), prev is None),
        grid=(NB,),
        in_specs=a_specs + g_specs + ([s_spec, m_spec] if extra else []),
        out_specs=[s_spec, m_spec],
        out_shape=[
            jax.ShapeDtypeStruct((QUART, QUART), F32),
            jax.ShapeDtypeStruct((NB, 2, BLK, BLK), F32),
        ],
        compiler_params=params(),
        cost_estimate=pl.CostEstimate(
            flops=2 * tok * QUART * (QUART + 2 * BLK), bytes_accessed=tok * QUART * 4 + 8 * QUART * QUART, transcendentals=0
        ),
        name="accumulate",
    )(*a_list, *g_list, *extra)


def split(value):
    high = value.astype(BF16)
    return high, (value - high.astype(F32)).astype(BF16)


def dot_split(a, b):
    a_high, a_low = split(a)
    b_high, b_low = split(b)
    wide = jnp.concatenate([b_high, b_low], axis=1)
    both = jnp.dot(
        jnp.concatenate([a_high, a_low], axis=1),
        jnp.concatenate([wide, wide], axis=0),
        preferred_element_type=F32,
    )
    return both[:, :BLK] + both[:, BLK:]


def dot_left(a, b):
    a_high, a_low = split(a)
    b_high, b_low = split(b)
    total = jnp.dot(
        jnp.concatenate([a_high, a_low], axis=1),
        jnp.concatenate([b_high, b_high], axis=0),
        preferred_element_type=F32,
    )
    return total + jnp.dot(a_high, b_low, preferred_element_type=F32)


def finish_kernel(core, s_prev, m_prev, *refs):
    keep, give, inv, upd = refs[6:]
    tok = refs[2].shape[0]
    late = [(refs[n // 2], (n % 2) * tok, refs[2 + n]) for n in range(4)]
    rows = lax.broadcasted_iota(jnp.int32, (BLK, BLK), 0)
    cols = lax.broadcasted_iota(jnp.int32, (BLK, BLK), 1)
    eye = (rows == cols).astype(F32)
    errs, scales = [], []
    for i in range(NB):
        blk = slice(i * BLK, (i + 1) * BLK)
        total = s_prev[blk, :]
        m_a, m_g = m_prev[i, 0], m_prev[i, 1]
        for a_ref, row, g_ref in late:
            a, g = a_ref[row : row + tok, blk], g_ref[:, blk]
            at = a.T
            total += jnp.dot(at, g_ref[...], preferred_element_type=F32)
            m_a += jnp.dot(at, a, preferred_element_type=F32)
            m_g += jnp.dot(g.T, g, preferred_element_type=F32)
        upd[blk, :] = total
        for m in (m_a, m_g):
            m = m * (1.0 / TOKENS) + DAMPING * eye
            bound = jnp.max(jnp.sum(jnp.abs(m), axis=0, keepdims=True), axis=1, keepdims=True)
            scale = 1.0 / bound
            errs.append(eye - m * scale)
            scales.append(scale)
    prods = [eye + e for e in errs]
    errs = [dot_split(e, e) for e in errs]
    for step in range(3):
        if step < 2:
            both = [dot_split(jnp.concatenate([p, e], axis=0), e) for p, e in zip(prods, errs)]
            prods = [p + t[:BLK] for p, t in zip(prods, both)]
            errs = [t[BLK:] for t in both]
        else:
            prods = [p + dot_split(p, e) for p, e in zip(prods, errs)]
    for n in range(2 * NB):
        inv[n] = prods[n] * scales[n]
    for i in range(NB):
        blk = slice(i * BLK, (i + 1) * BLK)
        upd[blk, :] = dot_left(inv[2 * i].T, upd[blk, :])
    for j in range(NB):
        blk = slice(j * BLK, (j + 1) * BLK)
        upd[:, blk] = dot_split(upd[:, blk], inv[2 * j + 1]) * (1.0 / math.sqrt(TOKENS))
    for out, parity in ((keep, core[0]), (give, 1 - core[0])):
        for b in range(2):
            start = pl.multiple_of((2 * b + parity) * OUT, 32)
            strip = upd[pl.ds(start, OUT), :]
            for j in range(4):
                piece = strip[:, j * OUT : (j + 1) * OUT]
                tail = piece[:, BLK:]
                packed = jnp.concatenate([tail[q * 40 : (q + 1) * 40] for q in range(4)], axis=1)
                packed = jnp.concatenate([packed, jnp.zeros((8, BLK), F32)], axis=0)
                out[b, j, :OUT, :] = piece[:, :BLK].astype(BF16)
                out[b, j, OUT:, :] = packed.astype(BF16)


def finish(core, sums, a_late, g_arrays):
    tok = a_late[0].shape[0] // 2

    def whole(shape):
        return pl.BlockSpec(shape, lambda i, c: (0,) * len(shape))

    out = jax.ShapeDtypeStruct((2, 4, PACK, BLK), BF16)
    return pl.pallas_call(
        finish_kernel,
        grid_spec=pltpu.PrefetchScalarGridSpec(
            num_scalar_prefetch=1,
            grid=(1,),
            in_specs=[whole(v.shape) for v in (*sums, *a_late)] + [whole((tok, QUART))] * 4,
            out_specs=[whole(out.shape)] * 2,
            scratch_shapes=[pltpu.VMEM((2 * NB, BLK, BLK), F32), pltpu.VMEM((QUART, QUART), F32)],
        ),
        out_shape=[out] * 2,
        compiler_params=params(),
        cost_estimate=pl.CostEstimate(flops=2 * 10**9, bytes_accessed=5 * 10**6, transcendentals=0),
        name="finish",
    )(core, *sums, *a_late, *g_arrays)


def unpack_kernel(src, dst):
    for l in range(8):
        tail = src[l, OUT:, :].astype(F32)
        ext = jnp.concatenate([tail[:40, q * 32 : (q + 1) * 32] for q in range(4)], axis=0)
        dst[l, :, :BLK] = src[l, :OUT, :]
        dst[l, :, BLK:] = ext.astype(BF16)


def unpack(packed):
    return pl.pallas_call(
        unpack_kernel,
        grid=(2,),
        in_specs=[pl.BlockSpec((8, PACK, BLK), lambda i: (i, 0, 0))],
        out_specs=pl.BlockSpec((8, OUT, OUT), lambda i: (i, 0, 0)),
        out_shape=jax.ShapeDtypeStruct((16, OUT, OUT), BF16),
        compiler_params=params(),
        name="unpack",
    )(packed)


def after(value, *done):
    return lax.optimization_barrier((value, *done))[0]


def local(acts, outgrads):
    d = lax.axis_index("dp")
    y, x, c = d // 8, (d // 2) % 4, d % 2
    place = jnp.stack([c, x]).astype(jnp.int32)
    a_now, g_now = acts[0], outgrads[0]
    tok = a_now.shape[0]

    g_left = send(columns(g_now, (x + 1) % 4, QUART), plus_x)
    g_right = send(columns(g_now, (x + 3) % 4, QUART), minus_x)
    g_far = send(columns(g_now, (x + 2) % 4, QUART), far_x)
    mate_all = jnp.concatenate(
        [send(columns(a_now, 2 * (1 - y) + c, QUART), swap_y), send(columns(a_now, 2 * (1 - y) + 1 - c, QUART), swap_y_core)], axis=0
    )
    own_all = jnp.concatenate(
        [columns(a_now, 2 * y + c, QUART), send(columns(a_now, 2 * y + 1 - c, QUART), swap_core)], axis=0
    )
    g_near = jnp.concatenate([columns(g_now, x, QUART), g_left, g_right], axis=0)
    g_mate = send(after(g_near, mate_all), swap_y)
    g_other = send(g_near, swap_core)
    own_left, own_right = send(own_all, plus_x), send(own_all, minus_x)
    mate_start = after(mate_all, g_far)
    mate_left, mate_right = send(mate_start, plus_x), send(mate_start, minus_x)
    g_far_mate = send(after(g_far, own_left, own_right), swap_y)
    own_far = send(own_left, plus_x)
    mate_far = send(mate_right, minus_x)
    g_mate_other = send(after(g_mate, own_left, own_right, mate_left, mate_right), swap_core)
    plan = [[(n, k * tok, tok), (n + 1, k * tok, tok)] for n in (0, 2) for k in range(3)]
    sums = accumulate(
        [own_all, own_left, own_right, mate_all, mate_left, mate_right], plan, [g_near, g_other, g_mate, g_mate_other]
    )
    g_late = []
    for block in lax.optimization_barrier((g_far, g_far_mate, mate_left, mate_right))[:2]:
        g_late += [block, send(block, swap_core)]
    keep, give = finish(place, sums, [own_far, mate_far], g_late)
    recv = send(give, swap_core)
    got = []
    for k, move in ((0, None), (1, plus_x), (3, minus_x), (2, far_x)):
        target = (x + k) % 4
        strip = jnp.where(
            target // 2 == c,
            lax.dynamic_index_in_dim(keep, target % 2, 0, False),
            lax.dynamic_index_in_dim(recv, target % 2, 0, False),
        )
        got.append(strip if move is None else send(strip, move))
    pieces = jnp.zeros((16, PACK, BLK), BF16)
    for k, strip in zip((0, 1, 3, 2), got):
        pieces = lax.dynamic_update_slice(pieces, strip, (((x + 4 - k) % 4) * 4, 0, 0))
    return unpack(lax.all_to_all(pieces, "owner", split_axis=0, concat_axis=0, tiled=True))


def solution(mesh):
    return jax.shard_map(
        local,
        mesh=mesh,
        in_specs=(P("owner", "dp", None), P("owner", "dp", None)),
        out_specs=P(None, "dp", "owner"),
        check_vma=False,
    )
```

```python
import functools
import math

import jax
import jax.numpy as jnp
from jax import lax
from jax.experimental import pallas as pl
from jax.experimental.pallas import tpu as pltpu
from jax.sharding import PartitionSpec as P

BLK = 128
DAMPING = 0.1
TOKENS = 4096
D = 2560
HALF = D // 2
QUART = D // 4
NB = QUART // BLK
OUT = 160
PACK = 208
AXES = ("dp", "owner")
F32 = jnp.float32
BF16 = jnp.bfloat16
HI = lax.Precision.HIGHEST
VMEM = 28 * 2**20


def params():
    return pltpu.CompilerParams(vmem_limit_bytes=VMEM)


def pairs(move):
    result = []
    for d in range(16):
        for o in range(16):
            y, x, c, p = move(d // 8, (d // 2) % 4, d % 2, o)
            result.append((d * 16 + o, (y * 8 + x * 2 + c) * 16 + p))
    return result


def send(value, move):
    return lax.ppermute(value, AXES, pairs(move))


def swap_y(y, x, c, o):
    return 1 - y, x, c, o


def swap_core(y, x, c, o):
    return y, x, 1 - c, o


def swap_y_core(y, x, c, o):
    return 1 - y, x, 1 - c, o


def plus_x(y, x, c, o):
    return y, (x + 1) % 4, c, o


def minus_x(y, x, c, o):
    return y, (x + 3) % 4, c, o


def far_x(y, x, c, o):
    return y, (x + 2) % 4, c, o


def columns(value, index, width):
    return lax.dynamic_slice(value, (0, index * width), (value.shape[0], width))


def accumulate_kernel(plan, n_g, first, *refs):
    n = len(plan)
    a_refs, g_refs, refs = refs[:n], refs[n : n + n_g], refs[n + n_g :]
    if not first:
        prev_s, prev_m, refs = refs[0], refs[1], refs[2:]
    s_ref, m_ref = refs
    col = pl.ds(pl.multiple_of(pl.program_id(0) * BLK, BLK), BLK)
    s = jnp.zeros((BLK, QUART), F32) if first else prev_s[...]
    m_a = jnp.zeros((BLK, BLK), F32) if first else prev_m[0, 0]
    m_g = jnp.zeros((BLK, BLK), F32) if first else prev_m[0, 1]
    for a_ref, parts in zip(a_refs, plan):
        row = 0
        for which, start, size in parts:
            a = a_ref[row : row + size, :]
            g = g_refs[which][start : start + size, :]
            part = g_refs[which][start : start + size, col]
            at = a.T
            both = jnp.dot(at, jnp.concatenate([g, a], axis=1), preferred_element_type=F32)
            s += both[:, :QUART]
            m_a += both[:, QUART:]
            m_g += jnp.dot(part.T, part, preferred_element_type=F32)
            row += size
    s_ref[...] = s
    m_ref[0, 0] = m_a
    m_ref[0, 1] = m_g


def accumulate(a_list, plan, g_list, prev=None):
    s_spec = pl.BlockSpec((BLK, QUART), lambda i: (i, 0))
    m_spec = pl.BlockSpec((1, 2, BLK, BLK), lambda i: (i, 0, 0, 0))
    a_specs = [pl.BlockSpec((a.shape[0], BLK), lambda i: (0, i)) for a in a_list]
    g_specs = [pl.BlockSpec(g.shape, lambda i: (0, 0)) for g in g_list]
    extra = [] if prev is None else list(prev)
    tok = sum(a.shape[0] for a in a_list)
    return pl.pallas_call(
        functools.partial(accumulate_kernel, plan, len(g_list), prev is None),
        grid=(NB,),
        in_specs=a_specs + g_specs + ([s_spec, m_spec] if extra else []),
        out_specs=[s_spec, m_spec],
        out_shape=[
            jax.ShapeDtypeStruct((QUART, QUART), F32),
            jax.ShapeDtypeStruct((NB, 2, BLK, BLK), F32),
        ],
        compiler_params=params(),
        cost_estimate=pl.CostEstimate(
            flops=2 * tok * QUART * (QUART + 2 * BLK), bytes_accessed=tok * QUART * 4 + 8 * QUART * QUART, transcendentals=0
        ),
        name="accumulate",
    )(*a_list, *g_list, *extra)


def split(value):
    high = value.astype(BF16)
    return high, (value - high.astype(F32)).astype(BF16)


def dot_split(a, b):
    a_high, a_low = split(a)
    b_high, b_low = split(b)
    wide = jnp.concatenate([b_high, b_low], axis=1)
    both = jnp.dot(
        jnp.concatenate([a_high, a_low], axis=1),
        jnp.concatenate([wide, wide], axis=0),
        preferred_element_type=F32,
    )
    return both[:, :BLK] + both[:, BLK:]


def dot_left(a, b):
    a_high, a_low = split(a)
    b_high, b_low = split(b)
    total = jnp.dot(
        jnp.concatenate([a_high, a_low], axis=1),
        jnp.concatenate([b_high, b_high], axis=0),
        preferred_element_type=F32,
    )
    return total + jnp.dot(a_high, b_low, preferred_element_type=F32)


def finish_kernel(core, s_prev, m_prev, *refs):
    give, inv, upd = refs[6:]
    tok = refs[2].shape[0]
    late = [(refs[n // 2], (n % 2) * tok, refs[2 + n]) for n in range(4)]
    rows = lax.broadcasted_iota(jnp.int32, (BLK, BLK), 0)
    cols = lax.broadcasted_iota(jnp.int32, (BLK, BLK), 1)
    eye = (rows == cols).astype(F32)
    errs, scales = [], []
    for i in range(NB):
        blk = slice(i * BLK, (i + 1) * BLK)
        total = s_prev[blk, :]
        m_a, m_g = m_prev[i, 0], m_prev[i, 1]
        for a_ref, row, g_ref in late:
            a, g = a_ref[row : row + tok, blk], g_ref[:, blk]
            at = a.T
            total += jnp.dot(at, g_ref[...], preferred_element_type=F32)
            m_a += jnp.dot(at, a, preferred_element_type=F32)
            m_g += jnp.dot(g.T, g, preferred_element_type=F32)
        upd[blk, :] = total
        for m in (m_a, m_g):
            m = m * (1.0 / TOKENS) + DAMPING * eye
            bound = jnp.max(jnp.sum(jnp.abs(m), axis=0, keepdims=True), axis=1, keepdims=True)
            scale = 1.0 / bound
            errs.append(eye - m * scale)
            scales.append(scale)
    prods = [eye + e for e in errs]
    errs = [dot_split(e, e) for e in errs]
    for step in range(3):
        if step < 2:
            both = [dot_split(jnp.concatenate([p, e], axis=0), e) for p, e in zip(prods, errs)]
            prods = [p + t[:BLK] for p, t in zip(prods, both)]
            errs = [t[BLK:] for t in both]
        else:
            prods = [p + dot_split(p, e) for p, e in zip(prods, errs)]
    for n in range(2 * NB):
        inv[n] = prods[n] * scales[n]
    for i in range(NB):
        blk = slice(i * BLK, (i + 1) * BLK)
        upd[blk, :] = dot_left(inv[2 * i].T, upd[blk, :])
    emit(give, 1 - core[0], upd, inv)


def keep_kernel(core, upd, inv, keep):
    emit(keep, core[0], upd, inv)


def emit(out, parity, upd, inv):
    for b in range(2):
        start = pl.multiple_of((2 * b + parity) * OUT, 32)
        left = upd[pl.ds(start, OUT), :]
        strip = jnp.concatenate(
            [dot_split(left[:, j * BLK : (j + 1) * BLK], inv[2 * j + 1]) for j in range(NB)], axis=1
        ) * (1.0 / math.sqrt(TOKENS))
        for j in range(4):
            piece = strip[:, j * OUT : (j + 1) * OUT]
            tail = piece[:, BLK:]
            packed = jnp.concatenate([tail[q * 40 : (q + 1) * 40] for q in range(4)], axis=1)
            packed = jnp.concatenate([packed, jnp.zeros((8, BLK), F32)], axis=0)
            out[b, j, :OUT, :] = piece[:, :BLK].astype(BF16)
            out[b, j, OUT:, :] = packed.astype(BF16)


def finish(core, sums, a_late, g_arrays):
    tok = a_late[0].shape[0] // 2

    def whole(shape):
        return pl.BlockSpec(shape, lambda i, c: (0,) * len(shape))

    out = jax.ShapeDtypeStruct((2, 4, PACK, BLK), BF16)
    inv = jax.ShapeDtypeStruct((2 * NB, BLK, BLK), F32)
    left = jax.ShapeDtypeStruct((QUART, QUART), F32)
    return pl.pallas_call(
        finish_kernel,
        grid_spec=pltpu.PrefetchScalarGridSpec(
            num_scalar_prefetch=1,
            grid=(1,),
            in_specs=[whole(v.shape) for v in (*sums, *a_late)] + [whole((tok, QUART))] * 4,
            out_specs=[whole(out.shape), whole(inv.shape), whole(left.shape)],
        ),
        out_shape=[out, inv, left],
        compiler_params=params(),
        cost_estimate=pl.CostEstimate(flops=2 * 10**9, bytes_accessed=5 * 10**6, transcendentals=0),
        name="finish",
    )(core, *sums, *a_late, *g_arrays)


def keep_strips(core, left, inv):
    vmem = pl.BlockSpec(memory_space=pltpu.VMEM)
    return pl.pallas_call(
        keep_kernel,
        in_specs=[pl.BlockSpec(memory_space=pltpu.SMEM), vmem, vmem],
        out_specs=vmem,
        out_shape=jax.ShapeDtypeStruct((2, 4, PACK, BLK), BF16),
        compiler_params=params(),
        cost_estimate=pl.CostEstimate(flops=10**9, bytes_accessed=5 * 10**6, transcendentals=0),
        name="keep",
    )(core, left, inv)


def unpack_kernel(src, dst):
    for l in range(8):
        tail = src[l, OUT:, :].astype(F32)
        ext = jnp.concatenate([tail[:40, q * 32 : (q + 1) * 32] for q in range(4)], axis=0)
        dst[l, :, :BLK] = src[l, :OUT, :]
        dst[l, :, BLK:] = ext.astype(BF16)


def unpack(packed):
    return pl.pallas_call(
        unpack_kernel,
        grid=(2,),
        in_specs=[pl.BlockSpec((8, PACK, BLK), lambda i: (i, 0, 0))],
        out_specs=pl.BlockSpec((8, OUT, OUT), lambda i: (i, 0, 0)),
        out_shape=jax.ShapeDtypeStruct((16, OUT, OUT), BF16),
        compiler_params=params(),
        name="unpack",
    )(packed)


def after(value, *done):
    return lax.optimization_barrier((value, *done))[0]


def local(acts, outgrads):
    d = lax.axis_index("dp")
    y, x, c = d // 8, (d // 2) % 4, d % 2
    place = jnp.stack([c, x]).astype(jnp.int32)
    a_now, g_now = acts[0], outgrads[0]
    tok = a_now.shape[0]

    g_left = send(columns(g_now, (x + 1) % 4, QUART), plus_x)
    g_right = send(columns(g_now, (x + 3) % 4, QUART), minus_x)
    g_far = send(columns(g_now, (x + 2) % 4, QUART), far_x)
    mate_all = jnp.concatenate(
        [send(columns(a_now, 2 * (1 - y) + c, QUART), swap_y), send(columns(a_now, 2 * (1 - y) + 1 - c, QUART), swap_y_core)], axis=0
    )
    own_all = jnp.concatenate(
        [columns(a_now, 2 * y + c, QUART), send(columns(a_now, 2 * y + 1 - c, QUART), swap_core)], axis=0
    )
    g_near = jnp.concatenate([columns(g_now, x, QUART), g_left, g_right], axis=0)
    g_mate = send(after(g_near, mate_all), swap_y)
    g_other = send(g_near, swap_core)
    own_left, own_right = send(own_all, plus_x), send(own_all, minus_x)
    mate_start = after(mate_all, g_far)
    mate_left, mate_right = send(mate_start, plus_x), send(mate_start, minus_x)
    g_far_mate = send(after(g_far, own_left, own_right), swap_y)
    own_far = send(own_left, plus_x)
    mate_far = send(mate_right, minus_x)
    g_mate_other = send(after(g_mate, own_left, own_right, mate_left, mate_right), swap_core)
    plan = [[(n, k * tok, tok), (n + 1, k * tok, tok)] for n in (0, 2) for k in range(3)]
    sums = accumulate(
        [own_all, own_left, own_right, mate_all, mate_left, mate_right], plan, [g_near, g_other, g_mate, g_mate_other]
    )
    g_late = []
    for block in lax.optimization_barrier((g_far, g_far_mate, mate_left, mate_right))[:2]:
        g_late += [block, send(block, swap_core)]
    give, inv, left = finish(place, sums, [own_far, mate_far], g_late)
    recv = send(give, swap_core)
    keep = keep_strips(place, left, inv)
    got = []
    for k, move in ((0, None), (1, plus_x), (3, minus_x), (2, far_x)):
        target = (x + k) % 4
        strip = jnp.where(
            target // 2 == c,
            lax.dynamic_index_in_dim(keep, target % 2, 0, False),
            lax.dynamic_index_in_dim(recv, target % 2, 0, False),
        )
        got.append(strip if move is None else send(strip, move))
    pieces = jnp.zeros((16, PACK, BLK), BF16)
    for k, strip in zip((0, 1, 3, 2), got):
        pieces = lax.dynamic_update_slice(pieces, strip, (((x + 4 - k) % 4) * 4, 0, 0))
    return unpack(lax.all_to_all(pieces, "owner", split_axis=0, concat_axis=0, tiled=True))


def solution(mesh):
    return jax.shard_map(
        local,
        mesh=mesh,
        in_specs=(P("owner", "dp", None), P("owner", "dp", None)),
        out_specs=P(None, "dp", "owner"),
        check_vma=False,
    )
```
